32 devices in a mesh: grp: 2 (over x), pts: 16 (over z, y, core).
Axes of the slice: x: 2, y: 2, z: 4, core: 2. Of those that a mesh axis runs over, the one named last changes fastest.
Arguments:
- coulomb: bfloat16 [4096, 4096], P('pts'), may hold values from -8 to 8, as said below
- chi_tiles: bfloat16 [16, 12, 5, 256, 256], P('pts', 'grp'), parts along dimension 1, may hold values from -0.0024414062 to 0.0024414062
- tile_offsets: int32 [16, 5], P('pts'), may hold values from -3 to 3, as said below
- tile_counts: int32 [16], P('pts'), may hold values from 1 to 5, as said below
Outputs:
- screened: float32 [4096, 768], P('pts', 'grp'), parts along dimension 1
The draws below stay inside these ranges and needn't reach their ends.
There are 2 independent parts, one for each index of `grp`. The reference program is written for one: setup_inputs(seed, part) draws one part's arguments, and reference() takes and returns one part's arrays. A program takes and returns all parts, laid end to end along the dimension named above; an argument that names none is the same for every part. Nothing has to cross between parts.
Inputs may be any that keep to these rules, and one draw needn't show every extreme that they name: coulomb is symmetric. `tile_offsets`: slots before tile_counts of a tile hold distinct offsets; slots from tile_counts on hold 0 and are ignored; some tile uses all 5 slots and reaches both -3 and 3. `tile_counts`: some tile has 5.
All inputs are finite; a program needn't handle non-finite values.
Results may differ from the reference program's by a relative error of at most 0.0019.
Values may be sent and summed in bfloat16 or wider, within the bound.
A program may use at most 64 MiB of HBM per device.

```python
import jax
import jax.numpy as jnp
from jax import lax

TILE = 256
SLAB = 64
NFREQ = 6
MAXT = 5
REACH = 3
NTILES = 16
POINTS = 4096
N_PTS = 16


def neighbour_lists(key):
    count_key, chosen_key, score_key = jax.random.split(key, 3)
    span_len = 2 * REACH + 1
    chosen = jax.random.randint(chosen_key, (), 0, NTILES)
    tile_ids = jnp.arange(NTILES)
    counts_drawn = jax.random.randint(count_key, (NTILES,), 1, MAXT + 1)
    counts_drawn = jnp.where(tile_ids == chosen, MAXT, counts_drawn).astype(jnp.int32)
    places = jnp.arange(span_len)
    scores = jax.random.randint(score_key, (NTILES, span_len), 0, 1 << 20) * span_len + places[None, :]
    forced = (jnp.abs(places - REACH) == REACH)[None, :] & (tile_ids == chosen)[:, None]
    scores = jnp.where(forced, places[None, :] - 2 * span_len, scores)
    ranking = jnp.argsort(scores, axis=1, stable=True)[:, :MAXT]
    offsets_drawn = ranking - REACH
    in_use = jnp.arange(MAXT)[None, :] < counts_drawn[:, None]
    offsets_drawn = jnp.where(in_use, offsets_drawn, 0)
    return (offsets_drawn.astype(jnp.int32), counts_drawn)


def draw_tile_offsets(key, part):
    return neighbour_lists(key)[0]


def draw_tile_counts(key, part):
    return neighbour_lists(key)[1]


def draw_coulomb(key, part):
    key = jax.random.fold_in(key, 7)
    base = jnp.clip(jax.random.normal(key, (POINTS, POINTS), jnp.float32), -5.5, 5.5)
    symmetric = (base + base.T) * 0.7071
    return symmetric.astype(jnp.bfloat16)


def levels(own_key, shape, cuts, least, top_value):
    level = 1.0
    for dim, parts in cuts:
        heights = jax.random.uniform(jax.random.fold_in(jax.random.fold_in(own_key, 6), dim), (parts,), jnp.float32, least / len(cuts), top_value / len(cuts))
        level = level * jnp.repeat(jnp.exp(heights), shape[dim] // parts).reshape((-1,) + (1,) * (len(shape) - 1 - dim))
    return level


def normal_values(rng, extent, deviation, limit, cuts=(), kind=jnp.bfloat16):
    values = jax.random.normal(rng, extent, jnp.float32) * deviation
    if len(cuts) > 0:
        values = levels(rng, extent, cuts, -0.22, 0.18) * values
    return jnp.clip(values, min=-limit, max=limit).astype(kind)


def setup_inputs(seed: int = 0, part: int = 0) -> dict:
    splits = jax.random.split(jax.random.key(seed), 5)
    own_keys = jax.random.split(jax.random.fold_in(splits[4], part), 5)
    coulomb = draw_coulomb(jax.random.fold_in(splits[4], 71), part)
    chi_tiles = normal_values(own_keys[1], (NTILES, NFREQ, MAXT, TILE, TILE), (MAXT * TILE * TILE * N_PTS) ** -0.5, 0.0024414062, ((0, 16),))
    tile_offsets = draw_tile_offsets(jax.random.fold_in(splits[4], 71), part)
    tile_counts = draw_tile_counts(jax.random.fold_in(splits[4], 71), part)
    return {"coulomb": coulomb, "chi_tiles": chi_tiles, "tile_offsets": tile_offsets, "tile_counts": tile_counts}


def reference(coulomb, chi_tiles, tile_offsets, tile_counts):
    v_slab = coulomb[:, :SLAB]
    slab_tiles = v_slab.reshape(NTILES, TILE, SLAB)
    tile_ids = jnp.arange(NTILES, dtype=jnp.int32)
    column_tiles = (tile_ids[:, None] + tile_offsets) % NTILES
    in_use = jnp.arange(MAXT, dtype=jnp.int32)[None, :] < tile_counts[:, None]

    def one_tile(inputs):
        blocks, columns, used = inputs
        fetched = slab_tiles[columns]
        fetched = jnp.where(used[:, None, None], fetched, jnp.zeros_like(fetched))
        return jnp.einsum('fkab,kbs->afs', blocks.astype(jnp.float32), fetched.astype(jnp.float32))

    induced = lax.map(one_tile, (chi_tiles, column_tiles, in_use))
    induced = induced.reshape(POINTS, NFREQ * SLAB).astype(jnp.bfloat16)
    product = jnp.dot(coulomb, induced, preferred_element_type=jnp.float32)
    return jnp.tile(v_slab.astype(jnp.float32), (1, NFREQ)) + product
```

```python
import functools

import jax
import jax.numpy as jnp
from jax import lax
from jax.experimental import pallas as pl
from jax.experimental.pallas import tpu as pltpu
from jax.sharding import PartitionSpec as P

SLAB = 64
REACH = 3
MESH = pl.DeviceIdType.MESH


def kernel(
    n, offsets_ref, counts_ref, coulomb_hbm, chi_hbm, out_ref,
    coulomb, chi, slabs, gathered,
    local_sem, halo_send, halo_recv, ring_send, ring_recv, sib_send, sib_recv,
):
    tile = coulomb.shape[0]
    nfreq, maxt = chi.shape[:2]
    chunks = gathered.shape[1]
    per = nfreq // chunks
    wide = per * SLAB
    chips = n // 2
    cols = 2 if n == 16 else 1
    height = chips // cols
    me = lax.axis_index("pts")
    core = me % 2
    sib = me + 1 - 2 * core
    chip = me // 2
    col = chip % cols
    up = chip // cols
    pos = col * height + up + col * (height - 1 - 2 * up)
    way = 1 - 2 * core

    def device_at(place, core):
        place = (place + 2 * chips) % chips
        col = place // height
        up = place % height
        return ((up + col * (height - 1 - 2 * up)) * cols + col) * 2 + core

    ring_to = device_at(pos + way, core)
    ring_from = device_at(pos - way, core)

    head = 128
    first = pltpu.make_async_copy(
        coulomb_hbm.at[:, pl.ds(0, head)], coulomb.at[:, pl.ds(0, head)], local_sem.at[0]
    )
    rest = pltpu.make_async_copy(
        coulomb_hbm.at[:, pl.ds(head, coulomb.shape[1] - head)],
        coulomb.at[:, pl.ds(head, coulomb.shape[1] - head)],
        local_sem.at[1],
    )
    chi_copies = [
        pltpu.make_async_copy(
            chi_hbm.at[0, pl.ds(j * per, per)], chi.at[pl.ds(j * per, per)], local_sem.at[2 + j]
        )
        for j in range(chunks)
    ]
    first.start()
    for c in chi_copies:
        c.start()
    rest.start()

    barrier = pltpu.get_barrier_semaphore()
    others = [d for d in range(-REACH, REACH + 1) if d != 0]
    for d in others:
        pl.semaphore_signal(
            barrier, inc=1, device_id={"pts": (me + d + n) % n}, device_id_type=MESH
        )
    for peer in (ring_to, ring_from):
        pl.semaphore_signal(barrier, inc=1, device_id={"pts": peer}, device_id_type=MESH)

    first.wait()
    own = coulomb[:, :SLAB]
    slabs[REACH] = own.astype(jnp.float32).T.astype(jnp.bfloat16)
    start = own.astype(jnp.float32)
    out_ref[...] = jnp.concatenate([start] * nfreq, axis=1)

    pl.semaphore_wait(barrier, len(others) + 2)

    def halo(d):
        return pltpu.make_async_remote_copy(
            src_ref=slabs.at[REACH],
            dst_ref=slabs.at[REACH - d],
            send_sem=halo_send.at[REACH + d],
            recv_sem=halo_recv.at[REACH - d],
            device_id={"pts": (me + d + n) % n},
            device_id_type=MESH,
        )

    for d in sorted(others, key=abs, reverse=True):
        halo(d).start()

    def to_ring(step, owner, j):
        return pltpu.make_async_remote_copy(
            src_ref=gathered.at[owner, j],
            dst_ref=gathered.at[owner, j],
            send_sem=ring_send.at[step, j],
            recv_sem=ring_recv.at[step, j],
            device_id={"pts": ring_to},
            device_id_type=MESH,
        )

    def to_sib(step, owner, j):
        return pltpu.make_async_remote_copy(
            src_ref=gathered.at[owner, j],
            dst_ref=gathered.at[owner, j],
            send_sem=sib_send.at[step, j],
            recv_sem=sib_recv.at[step, j],
            device_id={"pts": sib},
            device_id_type=MESH,
        )

    for d in others:
        halo(d).wait_recv()

    count = counts_ref[0]
    picked = []
    for k in range(maxt):
        slab = slabs[offsets_ref[0, k] + REACH]
        picked.append(jnp.where(k < count, slab, jnp.zeros_like(slab)))
    for j in range(chunks):
        chi_copies[j].wait()
        parts = []
        for f in range(j * per, (j + 1) * per):
            total = None
            for k in range(maxt):
                term = lax.dot_general(
                    chi[f, k], picked[k], (((1,), (1,)), ((), ())),
                    preferred_element_type=jnp.float32,
                )
                total = term if total is None else total + term
            parts.append(total)
        gathered[me, j] = jnp.concatenate(parts, axis=1).astype(jnp.bfloat16)
        to_ring(0, me, j).start()
        to_sib(0, me, j).start()

    rest.wait()

    def product(owner, j):
        columns = pl.ds(pl.multiple_of(owner * tile, tile), tile)
        return jnp.dot(coulomb[:, columns], gathered[owner, j], preferred_element_type=jnp.float32)

    for j in range(chunks):
        out_ref[:, j * wide : (j + 1) * wide] += product(me, j)

    def turn(step, carry):
        owner = device_at(pos - step * way, core)
        sib_owner = device_at(pos + (step - 1) * way, 1 - core)
        for j in range(chunks):
            to_ring(step - 1, owner, j).wait_recv()

            @pl.when(step < chips - 1)
            def _():
                to_ring(step, owner, j).start()

            to_sib(step, owner, j).start()
            to_sib(step - 1, sib_owner, j).wait_recv()
            out_ref[:, j * wide : (j + 1) * wide] += product(owner, j) + product(sib_owner, j)
        return carry

    lax.fori_loop(1, chips, turn, 0)

    last = device_at(pos + (chips - 1) * way, 1 - core)
    for j in range(chunks):
        to_sib(chips - 1, last, j).wait_recv()
        out_ref[:, j * wide : (j + 1) * wide] += product(last, j)

    for d in others:
        halo(d).wait_send()

    def settle(step, carry):
        for j in range(chunks):
            to_sib(step, me, j).wait_send()

            @pl.when(step < chips - 1)
            def _():
                to_ring(step, me, j).wait_send()
        return carry

    lax.fori_loop(0, chips, settle, 0)


def shards(n, coulomb, chi_tiles, tile_offsets, tile_counts):
    tile, points = coulomb.shape
    _, nfreq, maxt = chi_tiles.shape[:3]
    chunks = nfreq // 2
    chips = n // 2
    return pl.pallas_call(
        functools.partial(kernel, n),
        out_shape=jax.ShapeDtypeStruct((tile, nfreq * SLAB), jnp.float32),
        in_specs=[
            pl.BlockSpec(memory_space=pltpu.SMEM),
            pl.BlockSpec(memory_space=pltpu.SMEM),
            pl.BlockSpec(memory_space=pl.ANY),
            pl.BlockSpec(memory_space=pl.ANY),
        ],
        out_specs=pl.BlockSpec(memory_space=pltpu.VMEM),
        scratch_shapes=[
            pltpu.VMEM((tile, points), jnp.bfloat16),
            pltpu.VMEM(chi_tiles.shape[1:], jnp.bfloat16),
            pltpu.VMEM((2 * REACH + 1, SLAB, tile), jnp.bfloat16),
            pltpu.VMEM((n, chunks, tile, 2 * SLAB), jnp.bfloat16),
            pltpu.SemaphoreType.DMA((2 + chunks,)),
            pltpu.SemaphoreType.DMA((2 * REACH + 1,)),
            pltpu.SemaphoreType.DMA((2 * REACH + 1,)),
            pltpu.SemaphoreType.DMA((chips, chunks)),
            pltpu.SemaphoreType.DMA((chips, chunks)),
            pltpu.SemaphoreType.DMA((chips, chunks)),
            pltpu.SemaphoreType.DMA((chips, chunks)),
        ],
        compiler_params=pltpu.CompilerParams(
            collective_id=0, has_side_effects=True, vmem_limit_bytes=48 * 1024 * 1024
        ),
        cost_estimate=pl.CostEstimate(
            flops=2 * tile * points * nfreq * SLAB, bytes_accessed=6 * 1024 * 1024, transcendentals=0
        ),
    )(tile_offsets, tile_counts, coulomb, chi_tiles)


def solution(mesh):
    return jax.shard_map(
        functools.partial(shards, mesh.shape["pts"]),
        mesh=mesh,
        in_specs=(P("pts", None), P("pts", "grp", None, None, None), P("pts", None), P("pts")),
        out_specs=P("pts", "grp"),
        check_vma=False,
    )
```

```python
import functools

import jax
import jax.numpy as jnp
from jax import lax
from jax.experimental import pallas as pl
from jax.experimental.pallas import tpu as pltpu
from jax.sharding import PartitionSpec as P

SLAB = 64
REACH = 3
MESH = pl.DeviceIdType.MESH


def kernel(
    n, offsets_hbm, counts_hbm, coulomb_hbm, chi_hbm, out_ref,
    offsets_ref, counts_ref, coulomb, chi, slabs, gathered,
    local_sem, halo_send, halo_recv, ring_send, ring_recv, sib_send, sib_recv,
):
    tile = coulomb.shape[0]
    nfreq, maxt = chi.shape[:2]
    chunks = gathered.shape[1]
    per = nfreq // chunks
    wide = per * SLAB
    chips = n // 2
    cols = 2 if n == 16 else 1
    height = chips // cols
    me = lax.axis_index("pts")
    core = me % 2
    sib = me + 1 - 2 * core
    chip = me // 2
    col = chip % cols
    up = chip // cols
    pos = col * height + up + col * (height - 1 - 2 * up)
    way = 1 - 2 * core

    def device_at(place, core):
        place = (place + 2 * chips) % chips
        col = place // height
        up = place % height
        return ((up + col * (height - 1 - 2 * up)) * cols + col) * 2 + core

    ring_to = device_at(pos + way, core)
    ring_from = device_at(pos - way, core)

    head = 128
    first = pltpu.make_async_copy(
        coulomb_hbm.at[:, pl.ds(0, head)], coulomb.at[:, pl.ds(0, head)], local_sem.at[0]
    )
    rest = pltpu.make_async_copy(
        coulomb_hbm.at[:, pl.ds(head, coulomb.shape[1] - head)],
        coulomb.at[:, pl.ds(head, coulomb.shape[1] - head)],
        local_sem.at[1],
    )
    chi_copies = [
        pltpu.make_async_copy(
            chi_hbm.at[0, pl.ds(j * per, per)], chi.at[pl.ds(j * per, per)], local_sem.at[2 + j]
        )
        for j in range(chunks)
    ]
    table_copies = [
        pltpu.make_async_copy(offsets_hbm, offsets_ref, local_sem.at[2 + chunks]),
        pltpu.make_async_copy(counts_hbm, counts_ref, local_sem.at[3 + chunks]),
    ]
    first.start()
    for c in table_copies:
        c.start()
    for c in chi_copies:
        c.start()
    rest.start()

    barrier = pltpu.get_barrier_semaphore()
    others = [d for d in range(-REACH, REACH + 1) if d != 0]
    for d in others:
        pl.semaphore_signal(
            barrier, inc=1, device_id={"pts": (me + d + n) % n}, device_id_type=MESH
        )
    for peer in (ring_to, ring_from):
        pl.semaphore_signal(barrier, inc=1, device_id={"pts": peer}, device_id_type=MESH)

    first.wait()
    own = coulomb[:, :SLAB]
    slabs[REACH] = own.astype(jnp.float32).T.astype(jnp.bfloat16)
    start = own.astype(jnp.float32)
    out_ref[...] = jnp.concatenate([start] * nfreq, axis=1)

    pl.semaphore_wait(barrier, len(others) + 2)

    def halo(d):
        return pltpu.make_async_remote_copy(
            src_ref=slabs.at[REACH],
            dst_ref=slabs.at[REACH - d],
            send_sem=halo_send.at[REACH + d],
            recv_sem=halo_recv.at[REACH - d],
            device_id={"pts": (me + d + n) % n},
            device_id_type=MESH,
        )

    for d in sorted(others, key=abs, reverse=True):
        halo(d).start()

    def to_ring(stream, step, owner, j):
        return pltpu.make_async_remote_copy(
            src_ref=gathered.at[owner, j],
            dst_ref=gathered.at[owner, j],
            send_sem=ring_send.at[stream, step, j],
            recv_sem=ring_recv.at[stream, step, j],
            device_id={"pts": ring_to if stream == 0 else ring_from},
            device_id_type=MESH,
        )

    def to_sib(stream, step, owner, j):
        return pltpu.make_async_remote_copy(
            src_ref=gathered.at[owner, j],
            dst_ref=gathered.at[owner, j],
            send_sem=sib_send.at[stream, step, j],
            recv_sem=sib_recv.at[stream, step, j],
            device_id={"pts": sib},
            device_id_type=MESH,
        )

    for d in others:
        halo(d).wait_recv()

    for c in table_copies:
        c.wait()
    count = counts_ref[0]
    picked = []
    for k in range(maxt):
        slab = slabs[offsets_ref[0, k] + REACH]
        picked.append(jnp.where(k < count, slab, jnp.zeros_like(slab)))
    for j in range(chunks):
        chi_copies[j].wait()
        parts = []
        for f in range(j * per, (j + 1) * per):
            total = None
            for k in range(maxt):
                term = lax.dot_general(
                    chi[f, k], picked[k], (((1,), (1,)), ((), ())),
                    preferred_element_type=jnp.float32,
                )
                total = term if total is None else total + term
            parts.append(total)
        gathered[me, j] = jnp.concatenate(parts, axis=1).astype(jnp.bfloat16)
        to_ring(0, 0, me, j).start()
        to_ring(1, 0, me, j).start()
        to_sib(0, 0, me, j).start()

    rest.wait()

    def product(owner, j):
        columns = pl.ds(pl.multiple_of(owner * tile, tile), tile)
        return jnp.dot(coulomb[:, columns], gathered[owner, j], preferred_element_type=jnp.float32)

    for j in range(chunks):
        out_ref[:, j * wide : (j + 1) * wide] += product(me, j)

    half = chips // 2

    def turn(step, first, last):
        ahead = device_at(pos - step * way, core)
        behind = device_at(pos + step * way, core)
        sib_ahead = device_at(pos + (step - 1) * way, 1 - core)
        sib_behind = device_at(pos - (step - 1) * way, 1 - core)
        for j in range(chunks):
            to_ring(0, step - 1, ahead, j).wait_recv()
            if not last:
                to_ring(0, step, ahead, j).start()
            to_sib(0, step, ahead, j).start()
            total = product(ahead, j)
            if not last:
                to_ring(1, step - 1, behind, j).wait_recv()

                @pl.when(step < half - 1)
                def _():
                    to_ring(1, step, behind, j).start()

                to_sib(1, step, behind, j).start()
                total += product(behind, j)
            to_sib(0, step - 1, sib_ahead, j).wait_recv()
            total += product(sib_ahead, j)
            if not first:
                to_sib(1, step - 1, sib_behind, j).wait_recv()
                total += product(sib_behind, j)
            out_ref[:, j * wide : (j + 1) * wide] += total

    def middle(step, carry):
        turn(step, False, False)
        return carry

    turn(1, True, False)
    lax.fori_loop(2, half, middle, 0)
    turn(half, False, True)
    sib_ahead = device_at(pos + half * way, 1 - core)
    for j in range(chunks):
        to_sib(0, half, sib_ahead, j).wait_recv()
        out_ref[:, j * wide : (j + 1) * wide] += product(sib_ahead, j)

    for d in others:
        halo(d).wait_send()

    def settle(step, carry):
        for j in range(chunks):
            to_sib(0, step, me, j).wait_send()

            @pl.when(step < half)
            def _():
                to_ring(0, step, me, j).wait_send()

            @pl.when(step < half - 1)
            def _():
                to_ring(1, step, me, j).wait_send()

            @pl.when((step > 0) & (step < half))
            def _():
                to_sib(1, step, me, j).wait_send()

        return carry

    lax.fori_loop(0, half + 1, settle, 0)


def shards(n, coulomb, chi_tiles, tile_offsets, tile_counts):
    tile, points = coulomb.shape
    _, nfreq, maxt = chi_tiles.shape[:3]
    chunks = nfreq // 2
    chips = n // 2
    return pl.pallas_call(
        functools.partial(kernel, n),
        out_shape=jax.ShapeDtypeStruct((tile, nfreq * SLAB), jnp.float32),
        in_specs=[
            pl.BlockSpec(memory_space=pl.ANY),
            pl.BlockSpec(memory_space=pl.ANY),
            pl.BlockSpec(memory_space=pl.ANY),
            pl.BlockSpec(memory_space=pl.ANY),
        ],
        out_specs=pl.BlockSpec(memory_space=pltpu.VMEM),
        scratch_shapes=[
            pltpu.SMEM(tile_offsets.shape, jnp.int32),
            pltpu.SMEM(tile_counts.shape, jnp.int32),
            pltpu.VMEM((tile, points), jnp.bfloat16),
            pltpu.VMEM(chi_tiles.shape[1:], jnp.bfloat16),
            pltpu.VMEM((2 * REACH + 1, SLAB, tile), jnp.bfloat16),
            pltpu.VMEM((n, chunks, tile, 2 * SLAB), jnp.bfloat16),
            pltpu.SemaphoreType.DMA((4 + chunks,)),
            pltpu.SemaphoreType.DMA((2 * REACH + 1,)),
            pltpu.SemaphoreType.DMA((2 * REACH + 1,)),
            pltpu.SemaphoreType.DMA((2, chips // 2 + 1, chunks)),
            pltpu.SemaphoreType.DMA((2, chips // 2 + 1, chunks)),
            pltpu.SemaphoreType.DMA((2, chips // 2 + 1, chunks)),
            pltpu.SemaphoreType.DMA((2, chips // 2 + 1, chunks)),
        ],
        compiler_params=pltpu.CompilerParams(
            collective_id=0, has_side_effects=True, vmem_limit_bytes=60 * 1024 * 1024
        ),
        cost_estimate=pl.CostEstimate(
            flops=2 * tile * points * nfreq * SLAB, bytes_accessed=6 * 1024 * 1024, transcendentals=0
        ),
    )(tile_offsets, tile_counts, coulomb, chi_tiles)


def solution(mesh):
    return jax.shard_map(
        functools.partial(shards, mesh.shape["pts"]),
        mesh=mesh,
        in_specs=(P("pts", None), P("pts", "grp", None, None, None), P("pts", None), P("pts")),
        out_specs=P("pts", "grp"),
        check_vma=False,
    )
```

```python
import functools

import jax
import jax.numpy as jnp
from jax import lax
from jax.experimental import pallas as pl
from jax.experimental.pallas import tpu as pltpu
from jax.sharding import PartitionSpec as P

SLAB = 64
REACH = 3
SPLIT = 2
MESH = pl.DeviceIdType.MESH


def kernel(
    n, offsets_hbm, counts_hbm, coulomb_hbm, chi_hbm, out_ref,
    offsets_ref, counts_ref, coulomb, chi, slabs, gathered,
    local_sem, halo_send, halo_recv, ring_send, ring_recv, sib_send, sib_recv,
):
    tile = coulomb.shape[0]
    nfreq, maxt = chi.shape[:2]
    chunks = gathered.shape[1]
    per = nfreq // chunks
    wide = per * SLAB
    pieces = chunks * SPLIT
    chips = n // 2
    cols = 2 if n == 16 else 1
    height = chips // cols
    me = lax.axis_index("pts")
    core = me % 2
    sib = me + 1 - 2 * core
    chip = me // 2
    col = chip % cols
    up = chip // cols
    pos = col * height + up + col * (height - 1 - 2 * up)
    way = 1 - 2 * core

    def device_at(place, core):
        place = (place + 2 * chips) % chips
        col = place // height
        up = place % height
        return ((up + col * (height - 1 - 2 * up)) * cols + col) * 2 + core

    ring_to = device_at(pos + way, core)
    ring_from = device_at(pos - way, core)

    head = 128
    first = pltpu.make_async_copy(
        coulomb_hbm.at[:, pl.ds(0, head)], coulomb.at[:, pl.ds(0, head)], local_sem.at[0]
    )
    rest = pltpu.make_async_copy(
        coulomb_hbm.at[:, pl.ds(head, coulomb.shape[1] - head)],
        coulomb.at[:, pl.ds(head, coulomb.shape[1] - head)],
        local_sem.at[1],
    )
    chi_copies = [
        pltpu.make_async_copy(
            chi_hbm.at[0, pl.ds(j * per, per)], chi.at[pl.ds(j * per, per)], local_sem.at[2 + j]
        )
        for j in range(chunks)
    ]
    table_copies = [
        pltpu.make_async_copy(offsets_hbm, offsets_ref, local_sem.at[2 + chunks]),
        pltpu.make_async_copy(counts_hbm, counts_ref, local_sem.at[3 + chunks]),
    ]
    first.start()
    for c in table_copies:
        c.start()
    for c in chi_copies:
        c.start()
    rest.start()

    far = 3 * (2 * core - 1)
    barrier = pltpu.get_barrier_semaphore()
    peers = [sib, (me + 2) % n, (me - 2 + n) % n, (me + far + n) % n, ring_to, ring_from]
    for peer in peers:
        pl.semaphore_signal(barrier, inc=1, device_id={"pts": peer}, device_id_type=MESH)

    first.wait()
    own = coulomb[:, :SLAB]
    slabs[REACH] = own.astype(jnp.float32).T.astype(jnp.bfloat16)
    start = own.astype(jnp.float32)
    out_ref[...] = jnp.concatenate([start] * nfreq, axis=1)

    pl.semaphore_wait(barrier, len(peers))

    def slab_copy(sem, src, dst, peer):
        return pltpu.make_async_remote_copy(
            src_ref=slabs.at[src],
            dst_ref=slabs.at[dst],
            send_sem=halo_send.at[sem],
            recv_sem=halo_recv.at[sem],
            device_id={"pts": peer},
            device_id_type=MESH,
        )

    direct = [
        slab_copy(0, REACH, REACH - far, (me + far + n) % n),
        slab_copy(1, REACH, REACH - 2, (me + 2) % n),
        slab_copy(2, REACH, REACH + 2, (me - 2 + n) % n),
        slab_copy(3, REACH, REACH - 1 + 2 * core, sib),
    ]
    passed = [
        slab_copy(4, REACH - 2, REACH - 3 + 2 * core, sib),
        slab_copy(5, REACH + 2, REACH + 1 + 2 * core, sib),
    ]
    for c in direct:
        c.start()

    rows = tile // SPLIT

    def piece(owner, i):
        return gathered.at[owner, i // SPLIT, pl.ds(i % SPLIT * rows, rows)]

    def to_ring(stream, step, owner, j):
        return pltpu.make_async_remote_copy(
            src_ref=piece(owner, j),
            dst_ref=piece(owner, j),
            send_sem=ring_send.at[stream, step, j],
            recv_sem=ring_recv.at[stream, step, j],
            device_id={"pts": ring_to if stream == 0 else ring_from},
            device_id_type=MESH,
        )

    def to_sib(stream, step, owner, j):
        return pltpu.make_async_remote_copy(
            src_ref=piece(owner, j),
            dst_ref=piece(owner, j),
            send_sem=sib_send.at[stream, step, j],
            recv_sem=sib_recv.at[stream, step, j],
            device_id={"pts": sib},
            device_id_type=MESH,
        )

    direct[1].wait_recv()
    passed[0].start()
    direct[2].wait_recv()
    passed[1].start()
    for c in (direct[0], direct[3], *passed):
        c.wait_recv()

    for c in table_copies:
        c.wait()
    count = counts_ref[0]
    picked = []
    for k in range(maxt):
        slab = slabs[offsets_ref[0, k] + REACH]
        picked.append(jnp.where(k < count, slab, jnp.zeros_like(slab)))
    for i in range(pieces):
        j = i // SPLIT
        if i % SPLIT == 0:
            chi_copies[j].wait()
        band = pl.ds(i % SPLIT * rows, rows)
        parts = []
        for f in range(j * per, (j + 1) * per):
            total = None
            for k in range(maxt):
                term = lax.dot_general(
                    chi[f, k, band], picked[k], (((1,), (1,)), ((), ())),
                    preferred_element_type=jnp.float32,
                )
                total = term if total is None else total + term
            parts.append(total)
        gathered[me, j, band] = jnp.concatenate(parts, axis=1).astype(jnp.bfloat16)
        to_ring(0, 0, me, i).start()
        to_ring(1, 0, me, i).start()
        to_sib(0, 0, me, i).start()

    rest.wait()

    def product(owner, j):
        columns = pl.ds(pl.multiple_of(owner * tile, tile), tile)
        return jnp.dot(coulomb[:, columns], gathered[owner, j], preferred_element_type=jnp.float32)

    for j in range(chunks):
        out_ref[:, j * wide : (j + 1) * wide] += product(me, j)

    half = chips // 2

    def turn(step, first, last):
        ahead = device_at(pos - step * way, core)
        behind = device_at(pos + step * way, core)
        sib_ahead = device_at(pos + (step - 1) * way, 1 - core)
        sib_behind = device_at(pos - (step - 1) * way, 1 - core)
        for i in range(pieces):
            to_ring(0, step - 1, ahead, i).wait_recv()
            if not last:
                to_ring(0, step, ahead, i).start()
            to_sib(0, step, ahead, i).start()
            if not last:
                to_ring(1, step - 1, behind, i).wait_recv()

                @pl.when(step < half - 1)
                def _():
                    to_ring(1, step, behind, i).start()

                to_sib(1, step, behind, i).start()
            to_sib(0, step - 1, sib_ahead, i).wait_recv()
            if not first:
                to_sib(1, step - 1, sib_behind, i).wait_recv()
            if i % SPLIT == SPLIT - 1:
                j = i // SPLIT
                total = product(ahead, j) + product(sib_ahead, j)
                if not last:
                    total += product(behind, j)
                if not first:
                    total += product(sib_behind, j)
                out_ref[:, j * wide : (j + 1) * wide] += total

    def middle(step, carry):
        turn(step, False, False)
        return carry

    turn(1, True, False)
    lax.fori_loop(2, half, middle, 0)
    turn(half, False, True)
    sib_ahead = device_at(pos + half * way, 1 - core)
    for i in range(pieces):
        to_sib(0, half, sib_ahead, i).wait_recv()
        if i % SPLIT == SPLIT - 1:
            j = i // SPLIT
            out_ref[:, j * wide : (j + 1) * wide] += product(sib_ahead, j)

    for c in direct + passed:
        c.wait_send()

    def settle(step, carry):
        for i in range(pieces):
            to_sib(0, step, me, i).wait_send()

            @pl.when(step < half)
            def _():
                to_ring(0, step, me, i).wait_send()

            @pl.when(step < half - 1)
            def _():
                to_ring(1, step, me, i).wait_send()

            @pl.when((step > 0) & (step < half))
            def _():
                to_sib(1, step, me, i).wait_send()

        return carry

    lax.fori_loop(0, half + 1, settle, 0)


def shards(n, coulomb, chi_tiles, tile_offsets, tile_counts):
    tile, points = coulomb.shape
    _, nfreq, maxt = chi_tiles.shape[:3]
    chunks = nfreq // 2
    chips = n // 2
    return pl.pallas_call(
        functools.partial(kernel, n),
        out_shape=jax.ShapeDtypeStruct((tile, nfreq * SLAB), jnp.float32),
        in_specs=[
            pl.BlockSpec(memory_space=pl.ANY),
            pl.BlockSpec(memory_space=pl.ANY),
            pl.BlockSpec(memory_space=pl.ANY),
            pl.BlockSpec(memory_space=pl.ANY),
        ],
        out_specs=pl.BlockSpec(memory_space=pltpu.VMEM),
        scratch_shapes=[
            pltpu.SMEM(tile_offsets.shape, jnp.int32),
            pltpu.SMEM(tile_counts.shape, jnp.int32),
            pltpu.VMEM((tile, points), jnp.bfloat16),
            pltpu.VMEM(chi_tiles.shape[1:], jnp.bfloat16),
            pltpu.VMEM((2 * REACH + 1, SLAB, tile), jnp.bfloat16),
            pltpu.VMEM((n, chunks, tile, 2 * SLAB), jnp.bfloat16),
            pltpu.SemaphoreType.DMA((4 + chunks,)),
            pltpu.SemaphoreType.DMA((2 * REACH + 1,)),
            pltpu.SemaphoreType.DMA((2 * REACH + 1,)),
            pltpu.SemaphoreType.DMA((2, chips // 2 + 1, chunks * SPLIT)),
            pltpu.SemaphoreType.DMA((2, chips // 2 + 1, chunks * SPLIT)),
            pltpu.SemaphoreType.DMA((2, chips // 2 + 1, chunks * SPLIT)),
            pltpu.SemaphoreType.DMA((2, chips // 2 + 1, chunks * SPLIT)),
        ],
        compiler_params=pltpu.CompilerParams(
            collective_id=0, has_side_effects=True, vmem_limit_bytes=60 * 1024 * 1024
        ),
        cost_estimate=pl.CostEstimate(
            flops=2 * tile * points * nfreq * SLAB, bytes_accessed=6 * 1024 * 1024, transcendentals=0
        ),
    )(tile_offsets, tile_counts, coulomb, chi_tiles)


def solution(mesh):
    return jax.shard_map(
        functools.partial(shards, mesh.shape["pts"]),
        mesh=mesh,
        in_specs=(P("pts", None), P("pts", "grp", None, None, None), P("pts", None), P("pts")),
        out_specs=P("pts", "grp"),
        check_vma=False,
    )
```

```python
import functools

import jax
import jax.numpy as jnp
from jax import lax
from jax.experimental import pallas as pl
from jax.experimental.pallas import tpu as pltpu
from jax.sharding import PartitionSpec as P

SLAB = 64
REACH = 3
SPLIT = 2
MESH = pl.DeviceIdType.MESH


def kernel(
    n, offsets_hbm, counts_hbm, coulomb_hbm, chi_hbm, out_ref,
    offsets_ref, counts_ref, coulomb, chi, slabs, gathered,
    local_sem, halo_send, halo_recv, ring_send, ring_recv, sib_send, sib_recv, end_send, end_recv,
):
    tile = coulomb.shape[0]
    nfreq, maxt = chi.shape[:2]
    chunks = gathered.shape[1]
    per = nfreq // chunks
    wide = per * SLAB
    pieces = chunks * SPLIT
    chips = n // 2
    cols = 2 if n == 16 else 1
    height = chips // cols
    me = lax.axis_index("pts")
    core = me % 2
    sib = me + 1 - 2 * core
    chip = me // 2
    col = chip % cols
    up = chip // cols
    pos = col * height + up + col * (height - 1 - 2 * up)
    way = 1 - 2 * core

    def device_at(place, core):
        place = (place + 2 * chips) % chips
        col = place // height
        up = place % height
        return ((up + col * (height - 1 - 2 * up)) * cols + col) * 2 + core

    ring_to = device_at(pos + way, core)
    ring_from = device_at(pos - way, core)

    head = 128
    first = pltpu.make_async_copy(
        coulomb_hbm.at[:, pl.ds(0, head)], coulomb.at[:, pl.ds(0, head)], local_sem.at[0]
    )
    rest = pltpu.make_async_copy(
        coulomb_hbm.at[:, pl.ds(head, coulomb.shape[1] - head)],
        coulomb.at[:, pl.ds(head, coulomb.shape[1] - head)],
        local_sem.at[1],
    )
    chi_copies = [
        pltpu.make_async_copy(
            chi_hbm.at[0, pl.ds(j * per, per)], chi.at[pl.ds(j * per, per)], local_sem.at[2 + j]
        )
        for j in range(chunks)
    ]
    table_copies = [
        pltpu.make_async_copy(offsets_hbm, offsets_ref, local_sem.at[2 + chunks]),
        pltpu.make_async_copy(counts_hbm, counts_ref, local_sem.at[3 + chunks]),
    ]
    first.start()
    for c in table_copies:
        c.start()
    for c in chi_copies:
        c.start()
    rest.start()

    far = 3 * (2 * core - 1)
    barrier = pltpu.get_barrier_semaphore()
    peers = [sib, (me + 2) % n, (me - 2 + n) % n, (me + far + n) % n, ring_to, ring_from]
    for peer in peers:
        pl.semaphore_signal(barrier, inc=1, device_id={"pts": peer}, device_id_type=MESH)

    first.wait()
    own = coulomb[:, :SLAB]
    slabs[REACH] = own.astype(jnp.float32).T.astype(jnp.bfloat16)
    start = own.astype(jnp.float32)
    out_ref[...] = jnp.concatenate([start] * nfreq, axis=1)

    pl.semaphore_wait(barrier, len(peers))

    def slab_copy(sem, src, dst, peer):
        return pltpu.make_async_remote_copy(
            src_ref=slabs.at[src],
            dst_ref=slabs.at[dst],
            send_sem=halo_send.at[sem],
            recv_sem=halo_recv.at[sem],
            device_id={"pts": peer},
            device_id_type=MESH,
        )

    direct = [
        slab_copy(0, REACH, REACH - far, (me + far + n) % n),
        slab_copy(1, REACH, REACH - 2, (me + 2) % n),
        slab_copy(2, REACH, REACH + 2, (me - 2 + n) % n),
        slab_copy(3, REACH, REACH - 1 + 2 * core, sib),
    ]
    passed = [
        slab_copy(4, REACH - 2, REACH - 3 + 2 * core, sib),
        slab_copy(5, REACH + 2, REACH + 1 + 2 * core, sib),
    ]
    for c in direct:
        c.start()

    rows = tile // SPLIT

    def piece(owner, i):
        return gathered.at[owner, i // SPLIT, pl.ds(i % SPLIT * rows, rows)]

    def to_ring(stream, step, owner, j):
        return pltpu.make_async_remote_copy(
            src_ref=piece(owner, j),
            dst_ref=piece(owner, j),
            send_sem=ring_send.at[stream, step, j],
            recv_sem=ring_recv.at[stream, step, j],
            device_id={"pts": ring_to if stream == 0 else ring_from},
            device_id_type=MESH,
        )

    def to_sib(stream, step, owner):
        return pltpu.make_async_remote_copy(
            src_ref=gathered.at[owner],
            dst_ref=gathered.at[owner],
            send_sem=sib_send.at[stream, step],
            recv_sem=sib_recv.at[stream, step],
            device_id={"pts": sib},
            device_id_type=MESH,
        )

    def end_to_sib(owner, i):
        return pltpu.make_async_remote_copy(
            src_ref=piece(owner, i),
            dst_ref=piece(owner, i),
            send_sem=end_send.at[i],
            recv_sem=end_recv.at[i],
            device_id={"pts": sib},
            device_id_type=MESH,
        )

    direct[1].wait_recv()
    passed[0].start()
    direct[2].wait_recv()
    passed[1].start()
    for c in (direct[0], direct[3], *passed):
        c.wait_recv()

    for c in table_copies:
        c.wait()
    count = counts_ref[0]
    picked = []
    for k in range(maxt):
        slab = slabs[offsets_ref[0, k] + REACH]
        picked.append(jnp.where(k < count, slab, jnp.zeros_like(slab)))
    for i in range(pieces):
        j = i // SPLIT
        if i % SPLIT == 0:
            chi_copies[j].wait()
        band = pl.ds(i % SPLIT * rows, rows)
        parts = []
        for f in range(j * per, (j + 1) * per):
            total = None
            for k in range(maxt):
                term = lax.dot_general(
                    chi[f, k, band], picked[k], (((1,), (1,)), ((), ())),
                    preferred_element_type=jnp.float32,
                )
                total = term if total is None else total + term
            parts.append(total)
        gathered[me, j, band] = jnp.concatenate(parts, axis=1).astype(jnp.bfloat16)
        to_ring(0, 0, me, i).start()
        to_ring(1, 0, me, i).start()

    to_sib(0, 0, me).start()
    rest.wait()

    def product(owner, j):
        columns = pl.ds(pl.multiple_of(owner * tile, tile), tile)
        return jnp.dot(coulomb[:, columns], gathered[owner, j], preferred_element_type=jnp.float32)

    for j in range(chunks):
        out_ref[:, j * wide : (j + 1) * wide] += product(me, j)

    half = chips // 2

    def turn(step, first, last):
        ahead = device_at(pos - step * way, core)
        behind = device_at(pos + step * way, core)
        sib_ahead = device_at(pos + (step - 1) * way, 1 - core)
        sib_behind = device_at(pos - (step - 1) * way, 1 - core)
        for i in range(pieces):
            to_ring(0, step - 1, ahead, i).wait_recv()
            if last:
                end_to_sib(ahead, i).start()
            else:
                to_ring(0, step, ahead, i).start()
                to_ring(1, step - 1, behind, i).wait_recv()

                @pl.when(step < half - 1)
                def _():
                    to_ring(1, step, behind, i).start()

            if i % SPLIT == SPLIT - 1:
                j = i // SPLIT
                total = product(ahead, j)
                if not last:
                    total += product(behind, j)
                out_ref[:, j * wide : (j + 1) * wide] += total
            if i == pieces - 2:
                to_sib(0, step - 1, sib_ahead).wait_recv()
                if not first:
                    to_sib(1, step - 1, sib_behind).wait_recv()
                for j in range(chunks):
                    total = product(sib_ahead, j)
                    if not first:
                        total += product(sib_behind, j)
                    out_ref[:, j * wide : (j + 1) * wide] += total
        if not last:
            to_sib(0, step, ahead).start()
            to_sib(1, step, behind).start()

    def middle(step, carry):
        turn(step, False, False)
        return carry

    turn(1, True, False)
    lax.fori_loop(2, half, middle, 0)
    for c in direct + passed:
        c.wait_send()

    def settle(step, carry):
        to_sib(0, step, me).wait_send()

        @pl.when(step > 0)
        def _():
            to_sib(1, step, me).wait_send()

        for i in range(pieces):
            to_ring(0, step, me, i).wait_send()

            @pl.when(step < half - 1)
            def _():
                to_ring(1, step, me, i).wait_send()

        return carry

    lax.fori_loop(0, half - 1, settle, 0)
    turn(half, False, True)
    sib_ahead = device_at(pos + half * way, 1 - core)
    for i in range(pieces):
        end_to_sib(sib_ahead, i).wait_recv()
        if i % SPLIT == SPLIT - 1:
            j = i // SPLIT
            out_ref[:, j * wide : (j + 1) * wide] += product(sib_ahead, j)

    for i in range(pieces):
        end_to_sib(me, i).wait_send()

    settle(half - 1, 0)


def shards(n, coulomb, chi_tiles, tile_offsets, tile_counts):
    tile, points = coulomb.shape
    _, nfreq, maxt = chi_tiles.shape[:3]
    chunks = nfreq // 2
    chips = n // 2
    return pl.pallas_call(
        functools.partial(kernel, n),
        out_shape=jax.ShapeDtypeStruct((tile, nfreq * SLAB), jnp.float32),
        in_specs=[
            pl.BlockSpec(memory_space=pl.ANY),
            pl.BlockSpec(memory_space=pl.ANY),
            pl.BlockSpec(memory_space=pl.ANY),
            pl.BlockSpec(memory_space=pl.ANY),
        ],
        out_specs=pl.BlockSpec(memory_space=pltpu.VMEM),
        scratch_shapes=[
            pltpu.SMEM(tile_offsets.shape, jnp.int32),
            pltpu.SMEM(tile_counts.shape, jnp.int32),
            pltpu.VMEM((tile, points), jnp.bfloat16),
            pltpu.VMEM(chi_tiles.shape[1:], jnp.bfloat16),
            pltpu.VMEM((2 * REACH + 1, SLAB, tile), jnp.bfloat16),
            pltpu.VMEM((n, chunks, tile, 2 * SLAB), jnp.bfloat16),
            pltpu.SemaphoreType.DMA((4 + chunks,)),
            pltpu.SemaphoreType.DMA((2 * REACH + 1,)),
            pltpu.SemaphoreType.DMA((2 * REACH + 1,)),
            pltpu.SemaphoreType.DMA((2, chips // 2 + 1, chunks * SPLIT)),
            pltpu.SemaphoreType.DMA((2, chips // 2 + 1, chunks * SPLIT)),
            pltpu.SemaphoreType.DMA((2, chips // 2)),
            pltpu.SemaphoreType.DMA((2, chips // 2)),
            pltpu.SemaphoreType.DMA((chunks * SPLIT,)),
            pltpu.SemaphoreType.DMA((chunks * SPLIT,)),
        ],
        compiler_params=pltpu.CompilerParams(
            collective_id=0, has_side_effects=True, vmem_limit_bytes=60 * 1024 * 1024
        ),
        cost_estimate=pl.CostEstimate(
            flops=2 * tile * points * nfreq * SLAB, bytes_accessed=6 * 1024 * 1024, transcendentals=0
        ),
    )(tile_offsets, tile_counts, coulomb, chi_tiles)


def solution(mesh):
    return jax.shard_map(
        functools.partial(shards, mesh.shape["pts"]),
        mesh=mesh,
        in_specs=(P("pts", None), P("pts", "grp", None, None, None), P("pts", None), P("pts")),
        out_specs=P("pts", "grp"),
        check_vma=False,
    )
```

```python
import functools

import jax
import jax.numpy as jnp
from jax import lax
from jax.experimental import pallas as pl
from jax.experimental.pallas import tpu as pltpu
from jax.sharding import PartitionSpec as P

SLAB = 64
REACH = 3
SPLIT = 4
MESH = pl.DeviceIdType.MESH


def kernel(
    n, offsets_hbm, counts_hbm, coulomb_hbm, chi_hbm, out_ref,
    offsets_ref, counts_ref, coulomb, chi, slabs, gathered,
    local_sem, halo_send, halo_recv, ring_send, ring_recv, sib_send, sib_recv, end_send, end_recv,
):
    tile = coulomb.shape[0]
    nfreq, maxt = chi.shape[:2]
    chunks = gathered.shape[1]
    per = nfreq // chunks
    wide = per * SLAB
    pieces = chunks * SPLIT
    chips = n // 2
    cols = 2 if n == 16 else 1
    height = chips // cols
    me = lax.axis_index("pts")
    core = me % 2
    sib = me + 1 - 2 * core
    chip = me // 2
    col = chip % cols
    up = chip // cols
    pos = col * height + up + col * (height - 1 - 2 * up)
    way = 1 - 2 * core

    def device_at(place, core):
        place = (place + 2 * chips) % chips
        col = place // height
        up = place % height
        return ((up + col * (height - 1 - 2 * up)) * cols + col) * 2 + core

    ring_to = device_at(pos + way, core)
    ring_from = device_at(pos - way, core)

    head = 128
    first = pltpu.make_async_copy(
        coulomb_hbm.at[:, pl.ds(0, head)], coulomb.at[:, pl.ds(0, head)], local_sem.at[0]
    )
    rest = pltpu.make_async_copy(
        coulomb_hbm.at[:, pl.ds(head, coulomb.shape[1] - head)],
        coulomb.at[:, pl.ds(head, coulomb.shape[1] - head)],
        local_sem.at[1],
    )
    chi_copies = [
        pltpu.make_async_copy(
            chi_hbm.at[0, pl.ds(j * per, per)], chi.at[pl.ds(j * per, per)], local_sem.at[2 + j]
        )
        for j in range(chunks)
    ]
    table_copies = [
        pltpu.make_async_copy(offsets_hbm, offsets_ref, local_sem.at[2 + chunks]),
        pltpu.make_async_copy(counts_hbm, counts_ref, local_sem.at[3 + chunks]),
    ]
    first.start()
    for c in table_copies:
        c.start()
    for c in chi_copies:
        c.start()
    rest.start()

    far = 3 * (2 * core - 1)
    barrier = pltpu.get_barrier_semaphore()
    peers = [sib, (me + 2) % n, (me - 2 + n) % n, (me + far + n) % n, ring_to, ring_from]
    for peer in peers:
        pl.semaphore_signal(barrier, inc=1, device_id={"pts": peer}, device_id_type=MESH)

    first.wait()
    own = coulomb[:, :SLAB]
    slabs[REACH] = own.astype(jnp.float32).T.astype(jnp.bfloat16)
    start = own.astype(jnp.float32)
    out_ref[...] = jnp.concatenate([start] * nfreq, axis=1)

    pl.semaphore_wait(barrier, len(peers))

    def slab_copy(sem, src, dst, peer):
        return pltpu.make_async_remote_copy(
            src_ref=slabs.at[src],
            dst_ref=slabs.at[dst],
            send_sem=halo_send.at[sem],
            recv_sem=halo_recv.at[sem],
            device_id={"pts": peer},
            device_id_type=MESH,
        )

    direct = [
        slab_copy(0, REACH, REACH - far, (me + far + n) % n),
        slab_copy(1, REACH, REACH - 2, (me + 2) % n),
        slab_copy(2, REACH, REACH + 2, (me - 2 + n) % n),
        slab_copy(3, REACH, REACH - 1 + 2 * core, sib),
    ]
    passed = [
        slab_copy(4, REACH - 2, REACH - 3 + 2 * core, sib),
        slab_copy(5, REACH + 2, REACH + 1 + 2 * core, sib),
    ]
    for c in direct:
        c.start()

    rows = tile // SPLIT

    def piece(owner, i):
        return gathered.at[owner, i // SPLIT, pl.ds(i % SPLIT * rows, rows)]

    def to_ring(stream, step, owner, j):
        return pltpu.make_async_remote_copy(
            src_ref=piece(owner, j),
            dst_ref=piece(owner, j),
            send_sem=ring_send.at[stream, step, j],
            recv_sem=ring_recv.at[stream, step, j],
            device_id={"pts": ring_to if stream == 0 else ring_from},
            device_id_type=MESH,
        )

    def to_sib(stream, step, owner):
        return pltpu.make_async_remote_copy(
            src_ref=gathered.at[owner],
            dst_ref=gathered.at[owner],
            send_sem=sib_send.at[stream, step],
            recv_sem=sib_recv.at[stream, step],
            device_id={"pts": sib},
            device_id_type=MESH,
        )

    def end_to_sib(owner, i):
        return pltpu.make_async_remote_copy(
            src_ref=piece(owner, i),
            dst_ref=piece(owner, i),
            send_sem=end_send.at[i],
            recv_sem=end_recv.at[i],
            device_id={"pts": sib},
            device_id_type=MESH,
        )

    direct[1].wait_recv()
    passed[0].start()
    direct[2].wait_recv()
    passed[1].start()
    for c in (direct[0], direct[3], *passed):
        c.wait_recv()

    for c in table_copies:
        c.wait()
    count = counts_ref[0]
    picked = []
    for k in range(maxt):
        slab = slabs[offsets_ref[0, k] + REACH]
        picked.append(jnp.where(k < count, slab, jnp.zeros_like(slab)))
    for i in range(pieces):
        j = i // SPLIT
        if i % SPLIT == 0:
            chi_copies[j].wait()
        band = pl.ds(i % SPLIT * rows, rows)
        parts = []
        for f in range(j * per, (j + 1) * per):
            total = None
            for k in range(maxt):
                term = lax.dot_general(
                    chi[f, k, band], picked[k], (((1,), (1,)), ((), ())),
                    preferred_element_type=jnp.float32,
                )
                total = term if total is None else total + term
            parts.append(total)
        gathered[me, j, band] = jnp.concatenate(parts, axis=1).astype(jnp.bfloat16)
        to_ring(0, 0, me, i).start()
        to_ring(1, 0, me, i).start()

    to_sib(0, 0, me).start()
    rest.wait()

    def product(owner, j):
        columns = pl.ds(pl.multiple_of(owner * tile, tile), tile)
        return jnp.dot(coulomb[:, columns], gathered[owner, j], preferred_element_type=jnp.float32)

    for j in range(chunks):
        out_ref[:, j * wide : (j + 1) * wide] += product(me, j)

    half = chips // 2

    def turn(step, first, last):
        ahead = device_at(pos - step * way, core)
        behind = device_at(pos + step * way, core)
        sib_ahead = device_at(pos + (step - 1) * way, 1 - core)
        sib_behind = device_at(pos - (step - 1) * way, 1 - core)
        for i in range(pieces):
            to_ring(0, step - 1, ahead, i).wait_recv()
            if last:
                end_to_sib(ahead, i).start()
            else:
                to_ring(0, step, ahead, i).start()
                to_ring(1, step - 1, behind, i).wait_recv()

                @pl.when(step < half - 1)
                def _():
                    to_ring(1, step, behind, i).start()

            if i % SPLIT == SPLIT - 1:
                j = i // SPLIT
                total = product(ahead, j)
                if not last:
                    total += product(behind, j)
                out_ref[:, j * wide : (j + 1) * wide] += total
            if i == pieces - 2:
                to_sib(0, step - 1, sib_ahead).wait_recv()
                if not first:
                    to_sib(1, step - 1, sib_behind).wait_recv()
                for j in range(chunks):
                    total = product(sib_ahead, j)
                    if not first:
                        total += product(sib_behind, j)
                    out_ref[:, j * wide : (j + 1) * wide] += total
        if not last:
            to_sib(0, step, ahead).start()
            to_sib(1, step, behind).start()

    def middle(step, carry):
        turn(step, False, False)
        return carry

    turn(1, True, False)
    lax.fori_loop(2, half, middle, 0)
    for c in direct + passed:
        c.wait_send()

    def settle(step, carry):
        to_sib(0, step, me).wait_send()

        @pl.when(step > 0)
        def _():
            to_sib(1, step, me).wait_send()

        for i in range(pieces):
            to_ring(0, step, me, i).wait_send()

            @pl.when(step < half - 1)
            def _():
                to_ring(1, step, me, i).wait_send()

        return carry

    lax.fori_loop(0, half - 1, settle, 0)
    turn(half, False, True)
    sib_ahead = device_at(pos + half * way, 1 - core)
    for i in range(pieces):
        end_to_sib(sib_ahead, i).wait_recv()
        if i % SPLIT == SPLIT - 1:
            j = i // SPLIT
            out_ref[:, j * wide : (j + 1) * wide] += product(sib_ahead, j)

    for i in range(pieces):
        end_to_sib(me, i).wait_send()

    settle(half - 1, 0)


def shards(n, coulomb, chi_tiles, tile_offsets, tile_counts):
    tile, points = coulomb.shape
    _, nfreq, maxt = chi_tiles.shape[:3]
    chunks = 1
    chips = n // 2
    return pl.pallas_call(
        functools.partial(kernel, n),
        out_shape=jax.ShapeDtypeStruct((tile, nfreq * SLAB), jnp.float32),
        in_specs=[
            pl.BlockSpec(memory_space=pl.ANY),
            pl.BlockSpec(memory_space=pl.ANY),
            pl.BlockSpec(memory_space=pl.ANY),
            pl.BlockSpec(memory_space=pl.ANY),
        ],
        out_specs=pl.BlockSpec(memory_space=pltpu.VMEM),
        scratch_shapes=[
            pltpu.SMEM(tile_offsets.shape, jnp.int32),
            pltpu.SMEM(tile_counts.shape, jnp.int32),
            pltpu.VMEM((tile, points), jnp.bfloat16),
            pltpu.VMEM(chi_tiles.shape[1:], jnp.bfloat16),
            pltpu.VMEM((2 * REACH + 1, SLAB, tile), jnp.bfloat16),
            pltpu.VMEM((n, chunks, tile, nfreq // chunks * SLAB), jnp.bfloat16),
            pltpu.SemaphoreType.DMA((4 + chunks,)),
            pltpu.SemaphoreType.DMA((2 * REACH + 1,)),
            pltpu.SemaphoreType.DMA((2 * REACH + 1,)),
            pltpu.SemaphoreType.DMA((2, chips // 2 + 1, chunks * SPLIT)),
            pltpu.SemaphoreType.DMA((2, chips // 2 + 1, chunks * SPLIT)),
            pltpu.SemaphoreType.DMA((2, chips // 2)),
            pltpu.SemaphoreType.DMA((2, chips // 2)),
            pltpu.SemaphoreType.DMA((chunks * SPLIT,)),
            pltpu.SemaphoreType.DMA((chunks * SPLIT,)),
        ],
        compiler_params=pltpu.CompilerParams(
            collective_id=0, has_side_effects=True, vmem_limit_bytes=60 * 1024 * 1024
        ),
        cost_estimate=pl.CostEstimate(
            flops=2 * tile * points * nfreq * SLAB, bytes_accessed=6 * 1024 * 1024, transcendentals=0
        ),
    )(tile_offsets, tile_counts, coulomb, chi_tiles)


def solution(mesh):
    return jax.shard_map(
        functools.partial(shards, mesh.shape["pts"]),
        mesh=mesh,
        in_specs=(P("pts", None), P("pts", "grp", None, None, None), P("pts", None), P("pts")),
        out_specs=P("pts", "grp"),
        check_vma=False,
    )
```

```python
import functools

import jax
import jax.numpy as jnp
from jax import lax
from jax.experimental import pallas as pl
from jax.experimental.pallas import tpu as pltpu
from jax.sharding import PartitionSpec as P

SLAB = 64
REACH = 3
SPLIT = 4
MESH = pl.DeviceIdType.MESH


def kernel(
    n, offsets_hbm, counts_hbm, coulomb_hbm, chi_hbm, out_ref,
    offsets_ref, counts_ref, coulomb, chi, slabs, gathered,
    local_sem, halo_send, halo_recv, ring_send, ring_recv, sib_send, sib_recv, end_send, end_recv,
):
    tile = coulomb.shape[0]
    nfreq, maxt = chi.shape[:2]
    chunks = gathered.shape[1]
    per = nfreq // chunks
    wide = per * SLAB
    pieces = chunks * SPLIT
    chips = n // 2
    cols = 2 if n == 16 else 1
    height = chips // cols
    me = lax.axis_index("pts")
    core = me % 2
    sib = me + 1 - 2 * core
    chip = me // 2
    col = chip % cols
    up = chip // cols
    pos = col * height + up + col * (height - 1 - 2 * up)
    way = 1 - 2 * core

    def device_at(place, core):
        place = (place + 2 * chips) % chips
        col = place // height
        up = place % height
        return ((up + col * (height - 1 - 2 * up)) * cols + col) * 2 + core

    ring_to = device_at(pos + way, core)
    ring_from = device_at(pos - way, core)

    head = 128
    first = pltpu.make_async_copy(
        coulomb_hbm.at[:, pl.ds(0, head)], coulomb.at[:, pl.ds(0, head)], local_sem.at[0]
    )
    rest = pltpu.make_async_copy(
        coulomb_hbm.at[:, pl.ds(head, coulomb.shape[1] - head)],
        coulomb.at[:, pl.ds(head, coulomb.shape[1] - head)],
        local_sem.at[1],
    )
    chi_copies = [
        pltpu.make_async_copy(
            chi_hbm.at[0, pl.ds(j * per, per)], chi.at[pl.ds(j * per, per)], local_sem.at[2 + j]
        )
        for j in range(chunks)
    ]
    table_copies = [
        pltpu.make_async_copy(offsets_hbm, offsets_ref, local_sem.at[2 + chunks]),
        pltpu.make_async_copy(counts_hbm, counts_ref, local_sem.at[3 + chunks]),
    ]
    first.start()
    for c in table_copies:
        c.start()
    for c in chi_copies:
        c.start()
    rest.start()

    far = 3 * (2 * core - 1)
    barrier = pltpu.get_barrier_semaphore()
    peers = [sib, (me + 2) % n, (me - 2 + n) % n, (me + far + n) % n, ring_to, ring_from]
    for peer in peers:
        pl.semaphore_signal(barrier, inc=1, device_id={"pts": peer}, device_id_type=MESH)

    first.wait()
    own = coulomb[:, :SLAB]
    slabs[REACH] = own.astype(jnp.float32).T.astype(jnp.bfloat16)
    start = own.astype(jnp.float32)
    out_ref[...] = jnp.concatenate([start] * nfreq, axis=1)

    pl.semaphore_wait(barrier, len(peers))

    def slab_copy(sem, src, dst, peer):
        return pltpu.make_async_remote_copy(
            src_ref=slabs.at[src],
            dst_ref=slabs.at[dst],
            send_sem=halo_send.at[sem],
            recv_sem=halo_recv.at[sem],
            device_id={"pts": peer},
            device_id_type=MESH,
        )

    direct = [
        slab_copy(0, REACH, REACH - far, (me + far + n) % n),
        slab_copy(1, REACH, REACH - 2, (me + 2) % n),
        slab_copy(2, REACH, REACH + 2, (me - 2 + n) % n),
        slab_copy(3, REACH, REACH - 1 + 2 * core, sib),
    ]
    passed = [
        slab_copy(4, REACH - 2, REACH - 3 + 2 * core, sib),
        slab_copy(5, REACH + 2, REACH + 1 + 2 * core, sib),
    ]
    for c in direct:
        c.start()

    rows = tile // SPLIT

    def piece(owner, i):
        return gathered.at[owner, i // SPLIT, pl.ds(i % SPLIT * rows, rows)]

    def to_ring(stream, step, owner, j):
        return pltpu.make_async_remote_copy(
            src_ref=piece(owner, j),
            dst_ref=piece(owner, j),
            send_sem=ring_send.at[stream, step, j],
            recv_sem=ring_recv.at[stream, step, j],
            device_id={"pts": ring_to if stream == 0 else ring_from},
            device_id_type=MESH,
        )

    def to_sib(stream, step, owner):
        return pltpu.make_async_remote_copy(
            src_ref=gathered.at[owner],
            dst_ref=gathered.at[owner],
            send_sem=sib_send.at[stream, step],
            recv_sem=sib_recv.at[stream, step],
            device_id={"pts": sib},
            device_id_type=MESH,
        )

    def end_to_sib(owner, i):
        return pltpu.make_async_remote_copy(
            src_ref=piece(owner, i),
            dst_ref=piece(owner, i),
            send_sem=end_send.at[i],
            recv_sem=end_recv.at[i],
            device_id={"pts": sib},
            device_id_type=MESH,
        )

    direct[1].wait_recv()
    passed[0].start()
    direct[2].wait_recv()
    passed[1].start()
    for c in (direct[0], direct[3], *passed):
        c.wait_recv()

    for c in table_copies:
        c.wait()
    count = counts_ref[0]
    picked = []
    for k in range(maxt):
        slab = slabs[offsets_ref[0, k] + REACH]
        picked.append(jnp.where(k < count, slab, jnp.zeros_like(slab)))
    for i in range(pieces):
        j = i // SPLIT
        if i % SPLIT == 0:
            chi_copies[j].wait()
        band = pl.ds(i % SPLIT * rows, rows)
        parts = []
        for f in range(j * per, (j + 1) * per):
            total = None
            for k in range(maxt):
                term = lax.dot_general(
                    chi[f, k, band], picked[k], (((1,), (1,)), ((), ())),
                    preferred_element_type=jnp.float32,
                )
                total = term if total is None else total + term
            parts.append(total)
        gathered[me, j, band] = jnp.concatenate(parts, axis=1).astype(jnp.bfloat16)
        to_ring(0, 0, me, i).start()
        to_ring(1, 0, me, i).start()

    to_sib(0, 0, me).start()
    rest.wait()

    def product(owner, j):
        columns = pl.ds(pl.multiple_of(owner * tile, tile), tile)
        return jnp.dot(coulomb[:, columns], gathered[owner, j], preferred_element_type=jnp.float32)

    half = chips // 2

    def turn(step, first, last):
        ahead = device_at(pos - step * way, core)
        behind = device_at(pos + step * way, core)
        sib_ahead = device_at(pos + (step - 1) * way, 1 - core)
        sib_behind = device_at(pos - (step - 1) * way, 1 - core)
        for i in range(pieces):
            to_ring(0, step - 1, ahead, i).wait_recv()
            if last:
                end_to_sib(ahead, i).start()
            else:
                to_ring(0, step, ahead, i).start()
                to_ring(1, step - 1, behind, i).wait_recv()

                @pl.when(step < half - 1)
                def _():
                    to_ring(1, step, behind, i).start()

            if i % SPLIT == SPLIT - 1:
                j = i // SPLIT
                total = product(ahead, j)
                if not last:
                    total += product(behind, j)
                out_ref[:, j * wide : (j + 1) * wide] += total
            if i == pieces - 2:
                to_sib(0, step - 1, sib_ahead).wait_recv()
                if not first:
                    to_sib(1, step - 1, sib_behind).wait_recv()
                for j in range(chunks):
                    total = product(sib_ahead, j)
                    if first:
                        total += product(me, j)
                    if not first:
                        total += product(sib_behind, j)
                    out_ref[:, j * wide : (j + 1) * wide] += total
        if not last:
            to_sib(0, step, ahead).start()
            to_sib(1, step, behind).start()

    def middle(step, carry):
        turn(step, False, False)
        return carry

    turn(1, True, False)
    lax.fori_loop(2, half, middle, 0)
    for c in direct + passed:
        c.wait_send()

    def settle(step, carry):
        to_sib(0, step, me).wait_send()

        @pl.when(step > 0)
        def _():
            to_sib(1, step, me).wait_send()

        for i in range(pieces):
            to_ring(0, step, me, i).wait_send()

            @pl.when(step < half - 1)
            def _():
                to_ring(1, step, me, i).wait_send()

        return carry

    lax.fori_loop(0, half - 1, settle, 0)
    turn(half, False, True)
    sib_ahead = device_at(pos + half * way, 1 - core)
    for i in range(pieces):
        end_to_sib(sib_ahead, i).wait_recv()
        if i % SPLIT == SPLIT - 1:
            j = i // SPLIT
            out_ref[:, j * wide : (j + 1) * wide] += product(sib_ahead, j)

    for i in range(pieces):
        end_to_sib(me, i).wait_send()

    settle(half - 1, 0)


def shards(n, coulomb, chi_tiles, tile_offsets, tile_counts):
    tile, points = coulomb.shape
    _, nfreq, maxt = chi_tiles.shape[:3]
    chunks = 1
    chips = n // 2
    return pl.pallas_call(
        functools.partial(kernel, n),
        out_shape=jax.ShapeDtypeStruct((tile, nfreq * SLAB), jnp.float32),
        in_specs=[
            pl.BlockSpec(memory_space=pl.ANY),
            pl.BlockSpec(memory_space=pl.ANY),
            pl.BlockSpec(memory_space=pl.ANY),
            pl.BlockSpec(memory_space=pl.ANY),
        ],
        out_specs=pl.BlockSpec(memory_space=pltpu.VMEM),
        scratch_shapes=[
            pltpu.SMEM(tile_offsets.shape, jnp.int32),
            pltpu.SMEM(tile_counts.shape, jnp.int32),
            pltpu.VMEM((tile, points), jnp.bfloat16),
            pltpu.VMEM(chi_tiles.shape[1:], jnp.bfloat16),
            pltpu.VMEM((2 * REACH + 1, SLAB, tile), jnp.bfloat16),
            pltpu.VMEM((n, chunks, tile, nfreq // chunks * SLAB), jnp.bfloat16),
            pltpu.SemaphoreType.DMA((4 + chunks,)),
            pltpu.SemaphoreType.DMA((2 * REACH + 1,)),
            pltpu.SemaphoreType.DMA((2 * REACH + 1,)),
            pltpu.SemaphoreType.DMA((2, chips // 2 + 1, chunks * SPLIT)),
            pltpu.SemaphoreType.DMA((2, chips // 2 + 1, chunks * SPLIT)),
            pltpu.SemaphoreType.DMA((2, chips // 2)),
            pltpu.SemaphoreType.DMA((2, chips // 2)),
            pltpu.SemaphoreType.DMA((chunks * SPLIT,)),
            pltpu.SemaphoreType.DMA((chunks * SPLIT,)),
        ],
        compiler_params=pltpu.CompilerParams(
            collective_id=0, has_side_effects=True, vmem_limit_bytes=60 * 1024 * 1024
        ),
        cost_estimate=pl.CostEstimate(
            flops=2 * tile * points * nfreq * SLAB, bytes_accessed=6 * 1024 * 1024, transcendentals=0
        ),
    )(tile_offsets, tile_counts, coulomb, chi_tiles)


def solution(mesh):
    return jax.shard_map(
        functools.partial(shards, mesh.shape["pts"]),
        mesh=mesh,
        in_specs=(P("pts", None), P("pts", "grp", None, None, None), P("pts", None), P("pts")),
        out_specs=P("pts", "grp"),
        check_vma=False,
    )
```
